32 devices in a mesh: grp: 2 (over y), pair: 4 (over z), aux: 2 (over x), sub: 2 (over core).
Axes of the slice: x: 2, y: 2, z: 4, core: 2. Of those that a mesh axis runs over, the one named last changes fastest.
Arguments:
- blocks: bfloat16 [32, 512, 512], P(('grp', 'pair'), 'aux', 'sub'), parts along dimension 0, may hold values from -0.75 to 0.75
- need_lists: int32 [8, 8], P('grp'), parts along dimension 0, may hold values from 0 to 15, as said below
- pair_slots: int32 [160, 2], P(('grp', 'pair')), parts along dimension 0, may hold values from 0 to 7
- pno_class: int32 [160], P(('grp', 'pair')), parts along dimension 0, may hold values from 0 to 2
- projection: bfloat16 [160, 512, 256], P(('grp', 'pair'), None, 'sub'), parts along dimension 0, may hold values from -0.25 to 0.25
- amplitudes: bfloat16 [160, 256, 256], P(('grp', 'pair'), 'sub', 'aux'), parts along dimension 0, may hold values from -1.1953125 to 1.1953125
- pno_energy: float32 [160, 256], P(('grp', 'pair')), parts along dimension 0, may hold values from 0.2 to 3
- occ_energy: float32 [32], P('grp'), parts along dimension 0, may hold values from -1.5 to -0.2
Outputs:
- residual: bfloat16 [160, 256, 256], P(('grp', 'pair'), 'sub', 'aux'), parts along dimension 0
The draws below stay inside these ranges and needn't reach their ends.
There are 2 independent parts, one for each index of `grp`. The reference program is written for one: setup_inputs(seed, part) draws one part's arguments, and reference() takes and returns one part's arrays. A program takes and returns all parts, laid end to end along the dimension named above; each array names one. Nothing has to cross between parts.
Inputs may be any that keep to these rules, and one draw needn't show every extreme that they name: `need_lists`: row o lists 8 different orbitals; for each home h (orbitals h * 4 to h * 4 + 3) a row holds either none or exactly 2 of its orbitals.
All inputs are finite; a program needn't handle non-finite values.
Results may differ from the reference program's by a relative error of at most 0.0035.
Values may be sent and summed in bfloat16 or wider, within the bound.
A program may use at most 64 MiB of HBM per device.

```python
import jax
import jax.numpy as jnp
from jax import lax

NPNO = 256
MU = 512
Q_DEV = 256
ORBITALS_PER_UNIT = 4
PAIR_DEV = 20
NEED = 8
NOCC = 16
PAIRS = 80
QDOM = 512
N_PAIR = 4


def draw_need_lists(key, part):
    key = jax.random.fold_in(key, 7)
    homes_count = min(N_PAIR, 8)
    per_resident = NEED // homes_count

    def pick_locals(local_key):
        return jax.random.permutation(local_key, ORBITALS_PER_UNIT)[:per_resident]

    def one_owner(owner_key):
        resident_key, local_key, order_key = jax.random.split(owner_key, 3)
        homes = jax.random.permutation(resident_key, N_PAIR)[:homes_count]
        locals_picked = jax.vmap(pick_locals)(jax.random.split(local_key, homes_count))
        orbitals = (homes[:, None] * ORBITALS_PER_UNIT + locals_picked).reshape(-1)
        return jax.random.permutation(order_key, orbitals)
    return jax.vmap(one_owner)(jax.random.split(key, N_PAIR)).astype(jnp.int32)


def place_ends(drawn, own_key, least, largest):
    place = [jax.random.randint(jax.random.fold_in(own_key, axis), (), 0, length) for axis, length in enumerate(drawn.shape)]
    longest = drawn.shape.index(max(drawn.shape))
    next_to = place[:longest] + [(place[longest] + 1) % drawn.shape[longest]] + place[longest + 1:]
    return drawn.at[tuple(place)].set(least).at[tuple(next_to)].set(largest)


def level_of(own_key, shape, pieces, smallest, high):
    loudness, own = 1.0, jax.random.fold_in(own_key, 6)
    for dim, parts in pieces:
        steps = jnp.exp(jax.random.uniform(jax.random.fold_in(own, dim), (parts,), jnp.float32, smallest / len(pieces), high / len(pieces)))
        loudness = loudness * jnp.repeat(steps, shape[dim] // parts).reshape([-1 if axis == dim else 1 for axis in range(len(shape))])
    return loudness


def centred(rng, dims, spread, bound, shards=(), kind=jnp.bfloat16):
    values = spread * jax.random.normal(rng, dims, jnp.float32)
    if shards:
        values = values * level_of(rng, dims, shards, -0.22, 0.18)
    return jnp.clip(values, -bound, bound).astype(kind)


def setup_inputs(seed: int = 0, part: int = 0) -> dict:
    splits = jax.random.split(jax.random.key(seed), 9)
    part_keys = jax.random.split(jax.random.fold_in(splits[8], part), 9)
    return {
        "blocks": centred(part_keys[0], (NOCC, QDOM, MU), (Q_DEV // 4) ** -0.5, 0.75, ((0, 4), (1, 2), (2, 2))),
        "need_lists": draw_need_lists(jax.random.fold_in(jax.random.fold_in(splits[8], part), 71), part),
        "pair_slots": place_ends(jax.random.randint(part_keys[2], (PAIRS, 2), 0, NEED), jax.random.fold_in(part_keys[2], 1), 0, NEED - 1).astype(jnp.int32),
        "pno_class": place_ends(jax.random.randint(part_keys[3], (PAIRS,), 0, 3), jax.random.fold_in(part_keys[3], 1), 0, 2).astype(jnp.int32),
        "projection": centred(part_keys[4], (PAIRS, MU, NPNO), MU ** -0.5, 0.25, ((0, 4), (2, 2))),
        "amplitudes": centred(part_keys[5], (PAIRS, NPNO, NPNO), 0.2, 1.1953125, ((0, 4), (1, 2), (2, 2))),
        "pno_energy": jnp.clip(0.2 + 2.8 * jax.random.uniform(part_keys[6], (PAIRS, NPNO), jnp.float32) ** level_of(part_keys[6], (PAIRS, NPNO), ((0, 4),), -0.2, 0.2), 0.2, 3.0),
        "occ_energy": jnp.clip(jax.random.uniform(part_keys[7], (NOCC,), jnp.float32, -1.5, -0.2), -1.5, -0.2),
    }


def reference(blocks, need_lists, pair_slots, pno_class, projection, amplitudes, pno_energy, occ_energy):
    owner_of = (jnp.arange(PAIRS) // PAIR_DEV).astype(jnp.int32)
    orbit_i = need_lists[owner_of, pair_slots[:, 0]].astype(jnp.int32)
    orbit_j = need_lists[owner_of, pair_slots[:, 1]].astype(jnp.int32)
    energy_i = occ_energy[orbit_i]
    energy_j = occ_energy[orbit_j]

    def one_pair(items):
        first, second, basis, guess, energies, classes, shift = items
        block_i = lax.dynamic_index_in_dim(blocks, first, 0, keepdims=False)
        block_j = lax.dynamic_index_in_dim(blocks, second, 0, keepdims=False)
        first_side = jnp.dot(block_i, basis, preferred_element_type=jnp.float32).astype(jnp.bfloat16)
        second_side = jnp.dot(block_j, basis, preferred_element_type=jnp.float32).astype(jnp.bfloat16)
        exchange_term = jnp.dot(first_side.T, second_side, preferred_element_type=jnp.float32)
        live = (NPNO // 4) * jnp.where(classes == 0, 1, jnp.where(classes == 1, 2, 4))
        mask = (jnp.arange(NPNO) < live).astype(jnp.float32)
        denominator = energies[:, None] + energies[None, :] - shift
        value = mask[:, None] * mask[None, :] * (exchange_term + denominator * guess.astype(jnp.float32))
        return value.astype(jnp.bfloat16)

    return lax.map(one_pair, (orbit_i, orbit_j, projection, amplitudes, pno_energy, pno_class, energy_i + energy_j))
```

```python
import functools

import jax
import jax.numpy as jnp
from jax import lax
from jax.experimental import pallas as pl
from jax.experimental.pallas import tpu as pltpu
from jax.sharding import PartitionSpec as P


def body(blocks, need_lists, pair_slots, pno_class, projection, amplitudes, pno_energy, occ_energy):
    owner = lax.axis_index("pair")
    wanted = lax.dynamic_index_in_dim(need_lists, owner, 0, keepdims=False)
    everything = lax.all_gather(blocks, "pair", axis=0, tiled=True)
    packed_pairs = jnp.take(everything, wanted, axis=0)
    whole = lax.all_gather(packed_pairs, "sub", axis=2, tiled=True)
    slot_i = pair_slots[:, 0]
    slot_j = pair_slots[:, 1]
    left_rows = jnp.take(whole, slot_i, axis=0)
    right_rows = jnp.take(whole, slot_j, axis=0)
    first_side = jnp.einsum(
        "ltb,lba->lta", left_rows, projection, preferred_element_type=jnp.float32
    ).astype(jnp.bfloat16)
    second_half = jnp.einsum(
        "ltb,lba->lta", right_rows, projection, preferred_element_type=jnp.float32
    ).astype(jnp.bfloat16)
    second_side = lax.all_gather(second_half, "sub", axis=2, tiled=True)
    summed = lax.psum_scatter(
        jnp.einsum("pqa,pqb->bpa", first_side, second_side, preferred_element_type=jnp.float32),
        "aux",
        scatter_dimension=0,
        tiled=True,
    )
    exchange_term = jnp.transpose(summed, (1, 2, 0))
    half_width = projection.shape[2]
    col_width = summed.shape[0]
    row_start = lax.axis_index("sub") * half_width
    col_start = lax.axis_index("aux") * col_width
    energy_rows = lax.dynamic_slice_in_dim(pno_energy, row_start, half_width, 1)
    energy_cols = lax.dynamic_slice_in_dim(pno_energy, col_start, col_width, 1)
    shift = jnp.take(occ_energy, jnp.take(wanted, slot_i)) + jnp.take(
        occ_energy, jnp.take(wanted, slot_j)
    )
    denominator = energy_rows[:, :, None] + energy_cols[:, None, :] - shift[:, None, None]
    npno = pno_energy.shape[1]
    live = npno // 4 * jnp.where(pno_class == 0, 1, jnp.where(pno_class == 1, 2, 4))
    row_mask_table = ((row_start + jnp.arange(half_width))[None, :] < live[:, None]).astype(
        jnp.float32
    )
    mask_cols = ((col_start + jnp.arange(col_width))[None, :] < live[:, None]).astype(jnp.float32)
    value = (
        row_mask_table[:, :, None]
        * mask_cols[:, None, :]
        * (exchange_term + denominator * amplitudes.astype(jnp.float32))
    )
    return value.astype(jnp.bfloat16)


CHUNKS = 4
MESH = pl.DeviceIdType.MESH


def kernel(
    n_pair,
    blocks_ref,
    need_ref,
    slots_ref,
    class_ref,
    proj_ref,
    amp_ref,
    energy_ref,
    occ_ref,
    out_ref,
    *scratch,
):
    n_chunk = CHUNKS
    whole = scratch[:n_chunk]
    (packed, p_sub, p_aux, amp, acc, table, z_send, z_recv, x_send, x_recv, c_send, c_recv,
     d_send, d_recv, p_sem, l_sem) = scratch[n_chunk:]
    home = lax.axis_index("pair")
    x = lax.axis_index("aux")
    c = lax.axis_index("sub")
    per_home, q_dev, half_mu = blocks_ref.shape
    need = need_ref.shape[1]
    rows = q_dev // n_chunk
    n_occ = amp.shape[0]
    width = out_ref.shape[2]

    load_p = pltpu.make_async_copy(proj_ref, p_sub, l_sem.at[0])
    load_amp = pltpu.make_async_copy(amp_ref, amp, l_sem.at[1])
    load_aux = pltpu.make_async_copy(proj_ref, p_aux, l_sem.at[2])
    load_p.start()
    load_amp.start()

    barrier = pltpu.get_barrier_semaphore()
    for off in range(1, n_pair):
        pl.semaphore_signal(
            barrier, inc=1, device_id={"pair": lax.rem(home + off, n_pair)}, device_id_type=MESH
        )
    pl.semaphore_signal(barrier, inc=1, device_id={"aux": 1 - x}, device_id_type=MESH)
    pl.semaphore_signal(barrier, inc=1, device_id={"sub": 1 - c}, device_id_type=MESH)

    def pack(owner, store):
        seen = jnp.int32(0)
        local = [jnp.int32(0), jnp.int32(0)]
        for s in range(need):
            orbital = need_ref[owner, s] - home * per_home
            here = jnp.logical_and(orbital >= 0, orbital < per_home)
            for k in range(2):
                local[k] = jnp.where(jnp.logical_and(here, seen == k), orbital, local[k])
            seen = seen + here.astype(jnp.int32)
        for t in range(n_chunk):
            for k in range(2):
                store(t, k, blocks_ref[local[k], pl.ds(t * rows, rows), :])

    for off in range(1, n_pair):
        def store(t, k, value, off=off):
            packed[off - 1, t, k] = value
        pack(lax.rem(home + off, n_pair), store)

    pl.semaphore_wait(barrier, n_pair + 1)

    def z_copy(t, off):
        return pltpu.make_async_remote_copy(
            src_ref=packed.at[off - 1, t],
            dst_ref=whole[t].at[c, pl.ds(home * 2, 2), x],
            send_sem=z_send.at[t, off - 1],
            recv_sem=z_recv.at[t, home],
            device_id={"pair": lax.rem(home + off, n_pair)},
            device_id_type=MESH,
        )

    def z_wait(t, off):
        source = lax.rem(home + n_pair - off, n_pair)
        place = whole[t].at[c, pl.ds(source * 2, 2), x]
        pltpu.make_async_remote_copy(
            src_ref=place,
            dst_ref=place,
            send_sem=z_send.at[t, off - 1],
            recv_sem=z_recv.at[t, source],
            device_id={"pair": source},
            device_id_type=MESH,
        ).wait_recv()

    def hop(t, off, axis, to, half, send, recv, core):
        source = lax.rem(home + n_pair - off, n_pair)
        place = whole[t].at[core, pl.ds(source * 2, 2), half]
        return pltpu.make_async_remote_copy(
            src_ref=place,
            dst_ref=place,
            send_sem=send.at[t, source],
            recv_sem=recv.at[t, source],
            device_id={axis: to},
            device_id_type=MESH,
        )

    def x_out(t, off):
        return hop(t, off, "aux", 1 - x, x, x_send, x_recv, c)

    def x_in(t, off):
        return hop(t, off, "aux", 1 - x, 1 - x, x_send, x_recv, c)

    def c_out(t, off):
        return hop(t, off, "sub", 1 - c, x, c_send, c_recv, c)

    def c_in(t, off):
        return hop(t, off, "sub", 1 - c, x, c_send, c_recv, 1 - c)

    def d_out(t, off):
        return hop(t, off, "sub", 1 - c, 1 - x, d_send, d_recv, c)

    def d_in(t, off):
        return hop(t, off, "sub", 1 - c, 1 - x, d_send, d_recv, 1 - c)

    for t in range(n_chunk):
        for off in range(1, n_pair):
            z_copy(t, off).start()

    def store_own(t, k, value):
        whole[t][c, home * 2 + k, x] = value

    pack(home, store_own)
    for t in range(n_chunk):
        x_out(t, 0).start()
        c_out(t, 0).start()

    send_p = pltpu.make_async_remote_copy(
        src_ref=proj_ref,
        dst_ref=p_aux,
        send_sem=p_sem.at[0],
        recv_sem=p_sem.at[1],
        device_id={"sub": 1 - c},
        device_id_type=MESH,
    )

    @pl.when(x == c)
    def _():
        send_p.start()
        load_aux.start()

    for s in range(need):
        orbital = need_ref[home, s]
        origin = lax.div(orbital, jnp.int32(per_home))
        rank = jnp.int32(0)
        for before in range(s):
            rank = rank + (lax.div(need_ref[home, before], jnp.int32(per_home)) == origin).astype(jnp.int32)
        table[s] = origin * 2 + jnp.minimum(rank, 1)

    load_amp.wait()

    for i in range(n_occ):
        low, high = energy_ref[i : i + 1, :width], energy_ref[i : i + 1, width:]
        e_rows = jnp.where(c == 0, low, high)
        e_cols = jnp.where(x == 0, low, high)
        shift = occ_ref[need_ref[home, slots_ref[i, 0]]] + occ_ref[need_ref[home, slots_ref[i, 1]]]
        e_rows = jnp.transpose(jnp.broadcast_to(e_rows, (width, width)))
        acc[i] = (e_rows + e_cols - shift) * amp[i].astype(jnp.float32)

    load_p.wait()

    @pl.when(x == c)
    def _():
        send_p.wait_send()
        load_aux.wait()

    @pl.when(x != c)
    def _():
        send_p.wait_recv()

    group = 4 if n_occ % 4 == 0 else 1

    def side(t, slot, basis, i):
        total = None
        for core in range(2):
            left = whole[t][core, slot].reshape(2 * rows, half_mu)
            part = jnp.dot(
                left, basis[i, core * half_mu : (core + 1) * half_mu], preferred_element_type=jnp.float32
            )
            total = part if total is None else total + part
        return total.astype(jnp.bfloat16)

    def compute(t):
        def step(g, carry):
            for u in range(group):
                i = g * group + u
                first = side(t, table[slots_ref[i, 0]], p_sub, i)
                second = side(t, table[slots_ref[i, 1]], p_aux, i)
                value = acc[i] + lax.dot_general(
                    first, second, (((0,), (0,)), ((), ())), preferred_element_type=jnp.float32
                )
                if t < n_chunk - 1:
                    acc[i] = value
                else:
                    size = class_ref[i]
                    live = jnp.where(size == 0, width // 2, jnp.where(size == 1, width, 2 * width))
                    a = lax.broadcasted_iota(jnp.int32, (width, width), 0) + c * width
                    b = lax.broadcasted_iota(jnp.int32, (width, width), 1) + x * width
                    keep = jnp.logical_and(a < live, b < live)
                    out_ref[i] = jnp.where(keep, value, 0.0).astype(out_ref.dtype)
            return carry

        lax.fori_loop(0, n_occ // group, step, 0)

    def arrived(t):
        for off in range(n_pair):
            c_in(t, off).wait_recv()
            d_in(t, off).wait_recv()

    for t in range(n_chunk):
        for off in range(n_pair):
            if off:
                z_wait(t, off)
                x_out(t, off).start()
                c_out(t, off).start()
            if t:
                x_in(t - 1, off).wait_recv()
                d_out(t - 1, off).start()
        if t:
            arrived(t - 1)
            compute(t - 1)
    for off in range(n_pair):
        x_in(n_chunk - 1, off).wait_recv()
        d_out(n_chunk - 1, off).start()
    arrived(n_chunk - 1)
    compute(n_chunk - 1)

    for t in range(n_chunk):
        for off in range(n_pair):
            if off:
                z_copy(t, off).wait_send()
            x_out(t, off).wait_send()
            c_out(t, off).wait_send()
            d_out(t, off).wait_send()


def gathered(n_pair, blocks, need_lists, pair_slots, pno_class, projection, amplitudes, pno_energy, occ_energy):
    per_home, q_dev, half_mu = blocks.shape
    n_occ, mu, width = projection.shape
    rows = q_dev // CHUNKS
    dma = pltpu.SemaphoreType.DMA
    vmem = pl.BlockSpec(memory_space=pltpu.VMEM)
    smem = pl.BlockSpec(memory_space=pltpu.SMEM)
    hbm = pl.BlockSpec(memory_space=pl.ANY)
    scratch = [pltpu.VMEM((2, 2 * n_pair, 2, rows, half_mu), jnp.bfloat16) for _ in range(CHUNKS)]
    scratch += [
        pltpu.VMEM((n_pair - 1, CHUNKS, 2, rows, half_mu), jnp.bfloat16),
        pltpu.VMEM((n_occ, mu, width), jnp.bfloat16),
        pltpu.VMEM((n_occ, mu, width), jnp.bfloat16),
        pltpu.VMEM(amplitudes.shape, jnp.bfloat16),
        pltpu.VMEM(amplitudes.shape, jnp.float32),
        pltpu.SMEM((need_lists.shape[1],), jnp.int32),
        dma((CHUNKS, n_pair - 1)),
        dma((CHUNKS, n_pair)),
    ]
    scratch += [dma((CHUNKS, n_pair)) for _ in range(6)]
    scratch += [dma((2,)), dma((3,))]
    flops = 2 * n_occ * (2 * 2 * q_dev * mu * width + 2 * q_dev * width * width)
    return pl.pallas_call(
        functools.partial(kernel, n_pair),
        out_shape=jax.ShapeDtypeStruct(amplitudes.shape, jnp.bfloat16),
        in_specs=[vmem, smem, smem, smem, hbm, hbm, vmem, smem],
        out_specs=vmem,
        scratch_shapes=scratch,
        compiler_params=pltpu.CompilerParams(
            collective_id=0, has_side_effects=True, vmem_limit_bytes=40 * 1024 * 1024
        ),
        cost_estimate=pl.CostEstimate(flops=flops, bytes_accessed=8 * 1024 * 1024, transcendentals=0),
    )(blocks, need_lists, pair_slots, pno_class, projection, amplitudes, pno_energy, occ_energy)


def fits(mesh, blocks, need_lists, projection, amplitudes):
    n_pair = mesh.shape["pair"]
    if mesh.shape["aux"] != 2 or mesh.shape["sub"] != 2 or n_pair < 2:
        return False
    per_home, q_dev, half_mu = blocks.shape
    width = projection.shape[2]
    if amplitudes.shape[1:] != (width, width) or width % 128 or half_mu % 128 or q_dev % (16 * CHUNKS):
        return False
    held = 4 * 2 * n_pair * q_dev * half_mu * 2
    held += 2 * n_pair * q_dev * half_mu * 2 + 2 * projection.size * 2 + amplitudes.size * 10
    return held < 24 * 1024 * 1024


def solution(mesh):
    def one_device(blocks, need_lists, pair_slots, pno_class, projection, amplitudes, pno_energy, occ_energy):
        args = (blocks, need_lists, pair_slots, pno_class, projection, amplitudes, pno_energy, occ_energy)
        if fits(mesh, blocks, need_lists, projection, amplitudes):
            return gathered(mesh.shape["pair"], *args)
        return body(*args)

    placed = (
        P(("grp", "pair"), "aux", "sub"),
        P("grp", None),
        P(("grp", "pair"), None),
        P(("grp", "pair")),
        P(("grp", "pair"), None, "sub"),
        P(("grp", "pair"), "sub", "aux"),
        P(("grp", "pair"), None),
        P("grp"),
    )
    return jax.shard_map(
        one_device,
        mesh=mesh,
        in_specs=placed,
        out_specs=P(("grp", "pair"), "sub", "aux"),
        check_vma=False,
    )
```

```python
import functools

import jax
import jax.numpy as jnp
from jax import lax
from jax.experimental import pallas as pl
from jax.experimental.pallas import tpu as pltpu
from jax.sharding import PartitionSpec as P


def body(blocks, need_lists, pair_slots, pno_class, projection, amplitudes, pno_energy, occ_energy):
    owner = lax.axis_index("pair")
    wanted = lax.dynamic_index_in_dim(need_lists, owner, 0, keepdims=False)
    everything = lax.all_gather(blocks, "pair", axis=0, tiled=True)
    packed_pairs = jnp.take(everything, wanted, axis=0)
    whole = lax.all_gather(packed_pairs, "sub", axis=2, tiled=True)
    slot_i = pair_slots[:, 0]
    slot_j = pair_slots[:, 1]
    left_rows = jnp.take(whole, slot_i, axis=0)
    right_rows = jnp.take(whole, slot_j, axis=0)
    first_side = jnp.einsum(
        "ltb,lba->lta", left_rows, projection, preferred_element_type=jnp.float32
    ).astype(jnp.bfloat16)
    second_half = jnp.einsum(
        "ltb,lba->lta", right_rows, projection, preferred_element_type=jnp.float32
    ).astype(jnp.bfloat16)
    second_side = lax.all_gather(second_half, "sub", axis=2, tiled=True)
    summed = lax.psum_scatter(
        jnp.einsum("pqa,pqb->bpa", first_side, second_side, preferred_element_type=jnp.float32),
        "aux",
        scatter_dimension=0,
        tiled=True,
    )
    exchange_term = jnp.transpose(summed, (1, 2, 0))
    half_width = projection.shape[2]
    col_width = summed.shape[0]
    row_start = lax.axis_index("sub") * half_width
    col_start = lax.axis_index("aux") * col_width
    energy_rows = lax.dynamic_slice_in_dim(pno_energy, row_start, half_width, 1)
    energy_cols = lax.dynamic_slice_in_dim(pno_energy, col_start, col_width, 1)
    shift = jnp.take(occ_energy, jnp.take(wanted, slot_i)) + jnp.take(
        occ_energy, jnp.take(wanted, slot_j)
    )
    denominator = energy_rows[:, :, None] + energy_cols[:, None, :] - shift[:, None, None]
    npno = pno_energy.shape[1]
    live = npno // 4 * jnp.where(pno_class == 0, 1, jnp.where(pno_class == 1, 2, 4))
    row_mask_table = ((row_start + jnp.arange(half_width))[None, :] < live[:, None]).astype(
        jnp.float32
    )
    mask_cols = ((col_start + jnp.arange(col_width))[None, :] < live[:, None]).astype(jnp.float32)
    value = (
        row_mask_table[:, :, None]
        * mask_cols[:, None, :]
        * (exchange_term + denominator * amplitudes.astype(jnp.float32))
    )
    return value.astype(jnp.bfloat16)


CHUNKS = 2
MESH = pl.DeviceIdType.MESH


def kernel(
    n_pair,
    blocks_hbm,
    need_hbm,
    slots_hbm,
    class_hbm,
    proj_ref,
    amp_ref,
    energy_hbm,
    occ_hbm,
    out_ref,
    *scratch,
):
    n_chunk = CHUNKS
    whole = scratch[:n_chunk]
    (blocks_ref, need_ref, slots_ref, class_ref, energy_ref, occ_ref, packed, basis, amp, acc,
     result, table, z_send, z_recv, x_send, x_recv, c_send, c_recv, d_send, d_recv, s_sem,
     l_sem, o_sem) = scratch[n_chunk:]
    home = lax.axis_index("pair")
    x = lax.axis_index("aux")
    c = lax.axis_index("sub")
    per_home, q_dev, half_mu = blocks_ref.shape
    need = need_ref.shape[1]
    rows = q_dev // n_chunk
    n_mine = basis.shape[0]
    width = out_ref.shape[2]
    mine = c * n_mine
    theirs = (1 - c) * n_mine
    here_cols = pl.ds(pl.multiple_of(c * width, width), width)

    barrier = pltpu.get_barrier_semaphore()
    for off in range(1, n_pair):
        pl.semaphore_signal(
            barrier, inc=1, device_id={"pair": lax.rem(home + off, n_pair)}, device_id_type=MESH
        )
    pl.semaphore_signal(barrier, inc=1, device_id={"aux": 1 - x}, device_id_type=MESH)
    pl.semaphore_signal(barrier, inc=1, device_id={"sub": 1 - c}, device_id_type=MESH)

    loads = [
        pltpu.make_async_copy(source, target, l_sem.at[n])
        for n, (source, target) in enumerate(
            [
                (need_hbm, need_ref),
                (blocks_hbm, blocks_ref),
                (slots_hbm, slots_ref),
                (class_hbm, class_ref),
                (occ_hbm, occ_ref),
                (energy_hbm, energy_ref),
                (amp_ref.at[pl.ds(mine, n_mine)], amp.at[:, here_cols]),
                (proj_ref.at[pl.ds(mine, n_mine)], basis.at[:, :, here_cols]),
            ]
        )
    ]
    for load in loads:
        load.start()
    loads[0].wait()
    loads[1].wait()

    def pack(owner, store):
        seen = jnp.int32(0)
        local = [jnp.int32(0), jnp.int32(0)]
        for s in range(need):
            orbital = need_ref[owner, s] - home * per_home
            here = jnp.logical_and(orbital >= 0, orbital < per_home)
            for k in range(2):
                local[k] = jnp.where(jnp.logical_and(here, seen == k), orbital, local[k])
            seen = seen + here.astype(jnp.int32)
        for t in range(n_chunk):
            for k in range(2):
                store(t, k, blocks_ref[local[k], pl.ds(t * rows, rows), :])

    for off in range(1, n_pair):
        def store(t, k, value, off=off):
            packed[off - 1, t, k] = value
        pack(lax.rem(home + off, n_pair), store)

    def store_own(t, k, value):
        whole[t][c, home * 2 + k, x] = value

    pack(home, store_own)

    pl.semaphore_wait(barrier, n_pair + 1)

    def z_copy(t, off):
        return pltpu.make_async_remote_copy(
            src_ref=packed.at[off - 1, t],
            dst_ref=whole[t].at[c, pl.ds(home * 2, 2), x],
            send_sem=z_send.at[t, off - 1],
            recv_sem=z_recv.at[t, home],
            device_id={"pair": lax.rem(home + off, n_pair)},
            device_id_type=MESH,
        )

    def z_wait(t, off):
        source = lax.rem(home + n_pair - off, n_pair)
        place = whole[t].at[c, pl.ds(source * 2, 2), x]
        pltpu.make_async_remote_copy(
            src_ref=place,
            dst_ref=place,
            send_sem=z_send.at[t, off - 1],
            recv_sem=z_recv.at[t, source],
            device_id={"pair": source},
            device_id_type=MESH,
        ).wait_recv()

    def hop(t, off, axis, to, half, send, recv, core):
        source = lax.rem(home + n_pair - off, n_pair)
        place = whole[t].at[core, pl.ds(source * 2, 2), half]
        return pltpu.make_async_remote_copy(
            src_ref=place,
            dst_ref=place,
            send_sem=send.at[t, source],
            recv_sem=recv.at[t, source],
            device_id={axis: to},
            device_id_type=MESH,
        )

    def x_out(t, off):
        return hop(t, off, "aux", 1 - x, x, x_send, x_recv, c)

    def x_in(t, off):
        return hop(t, off, "aux", 1 - x, 1 - x, x_send, x_recv, c)

    def c_out(t, off):
        return hop(t, off, "sub", 1 - c, x, c_send, c_recv, c)

    def c_in(t, off):
        return hop(t, off, "sub", 1 - c, x, c_send, c_recv, 1 - c)

    def d_out(t, off):
        return hop(t, off, "sub", 1 - c, 1 - x, d_send, d_recv, c)

    def d_in(t, off):
        return hop(t, off, "sub", 1 - c, 1 - x, d_send, d_recv, 1 - c)

    def swap(n, source, target):
        return pltpu.make_async_remote_copy(
            src_ref=source,
            dst_ref=target,
            send_sem=s_sem.at[n, 0],
            recv_sem=s_sem.at[n, 1],
            device_id={"sub": 1 - c},
            device_id_type=MESH,
        )

    for t in range(n_chunk):
        for off in range(1, n_pair):
            z_copy(t, off).start()
        x_out(t, 0).start()
    swaps = [
        swap(0, amp_ref.at[pl.ds(theirs, n_mine)], amp.at[:, here_cols]),
        swap(1, proj_ref.at[pl.ds(theirs, n_mine)], basis.at[:, :, here_cols]),
    ]
    for copy in swaps:
        copy.start()
    for t in range(n_chunk):
        c_out(t, 0).start()

    for s in range(need):
        orbital = need_ref[home, s]
        origin = lax.div(orbital, jnp.int32(per_home))
        rank = jnp.int32(0)
        for before in range(s):
            rank = rank + (lax.div(need_ref[home, before], jnp.int32(per_home)) == origin).astype(jnp.int32)
        table[s] = origin * 2 + jnp.minimum(rank, 1)

    for load in loads[2:]:
        load.wait()
    for copy in swaps:
        copy.wait()

    for i in range(n_mine):
        p = mine + i
        energy = jnp.where(c == 0, energy_ref[i : i + 1, :], energy_ref[n_mine + i : n_mine + i + 1, :])
        cols = jnp.where(x == 0, energy[:, :width], energy[:, width:])
        shift = occ_ref[need_ref[home, slots_ref[0, p]]] + occ_ref[need_ref[home, slots_ref[1, p]]]
        for half in range(2):
            part = slice(half * width, (half + 1) * width)
            down = jnp.transpose(jnp.broadcast_to(energy[:, part], (width, width)))
            acc[i, part] = (down + cols - shift) * amp[i, part].astype(jnp.float32)

    group = 2 if n_mine % 2 == 0 else 1

    def compute(t, i):
        p = mine + i
        slot_i = table[slots_ref[0, p]]
        slot_j = table[slots_ref[1, p]]
        total = None
        for core in range(2):
            left = jnp.concatenate(
                [
                    whole[t][core, slot_i].reshape(2 * rows, half_mu),
                    whole[t][core, slot_j].reshape(2 * rows, half_mu),
                ],
                axis=0,
            )
            part = jnp.dot(
                left, basis[i, core * half_mu : (core + 1) * half_mu], preferred_element_type=jnp.float32
            )
            total = part if total is None else total + part
        first = total[: 2 * rows].astype(jnp.bfloat16)
        second = total[2 * rows :]
        second = jnp.where(x == 0, second[:, :width], second[:, width:]).astype(jnp.bfloat16)
        value = acc[i] + lax.dot_general(
            first, second, (((0,), (0,)), ((), ())), preferred_element_type=jnp.float32
        )
        if t < n_chunk - 1:
            acc[i] = value
            return
        size = class_ref[p]
        live = jnp.where(size == 0, width // 2, jnp.where(size == 1, width, 2 * width))
        a = lax.broadcasted_iota(jnp.int32, value.shape, 0)
        b = lax.broadcasted_iota(jnp.int32, value.shape, 1) + x * width
        keep = jnp.logical_and(a < live, b < live)
        value = jnp.where(keep, value, 0.0).astype(out_ref.dtype)
        result[i, 0] = value[:width]
        result[i, 1] = value[width:]

    def keep_rows(g):
        return pltpu.make_async_copy(
            result.at[pl.ds(g * group, group), c],
            out_ref.at[pl.ds(mine + g * group, group)],
            o_sem.at[0, g],
        )

    def give_rows(g):
        return pltpu.make_async_remote_copy(
            src_ref=result.at[pl.ds(g * group, group), 1 - c],
            dst_ref=out_ref.at[pl.ds(mine + g * group, group)],
            send_sem=o_sem.at[1, g],
            recv_sem=o_sem.at[2, g],
            device_id={"sub": 1 - c},
            device_id_type=MESH,
        )

    def take_rows(g):
        place = out_ref.at[pl.ds(theirs + g * group, group)]
        return pltpu.make_async_remote_copy(
            src_ref=place,
            dst_ref=place,
            send_sem=o_sem.at[1, g],
            recv_sem=o_sem.at[2, g],
            device_id={"sub": 1 - c},
            device_id_type=MESH,
        )

    def compute_all(t):
        def step(g, carry):
            for u in range(group):
                compute(t, g * group + u)
            if t == n_chunk - 1:
                keep_rows(g).start()
                give_rows(g).start()
            return carry

        lax.fori_loop(0, n_mine // group, step, 0)

    def arrived(t):
        for off in range(n_pair):
            c_in(t, off).wait_recv()
            d_in(t, off).wait_recv()

    for t in range(n_chunk):
        for off in range(n_pair):
            if off:
                z_wait(t, off)
                x_out(t, off).start()
                c_out(t, off).start()
            if t:
                x_in(t - 1, off).wait_recv()
                d_out(t - 1, off).start()
        if t:
            arrived(t - 1)
            compute_all(t - 1)
    for off in range(n_pair):
        x_in(n_chunk - 1, off).wait_recv()
        d_out(n_chunk - 1, off).start()
    arrived(n_chunk - 1)
    compute_all(n_chunk - 1)

    for t in range(n_chunk):
        for off in range(n_pair):
            if off:
                z_copy(t, off).wait_send()
            x_out(t, off).wait_send()
            c_out(t, off).wait_send()
            d_out(t, off).wait_send()
    for g in range(n_mine // group):
        keep_rows(g).wait()
        give_rows(g).wait_send()
        take_rows(g).wait_recv()


def gathered(n_pair, blocks, need_lists, pair_slots, pno_class, projection, amplitudes, pno_energy, occ_energy):
    per_home, q_dev, half_mu = blocks.shape
    n_occ, mu, width = projection.shape
    rows = q_dev // CHUNKS
    dma = pltpu.SemaphoreType.DMA
    hbm = pl.BlockSpec(memory_space=pltpu.HBM)
    scratch = [pltpu.VMEM((2, 2 * n_pair, 2, rows, half_mu), jnp.bfloat16) for _ in range(CHUNKS)]
    n_mine = n_occ // 2
    scratch += [
        pltpu.VMEM(blocks.shape, blocks.dtype),
        pltpu.SMEM(need_lists.shape, jnp.int32),
        pltpu.SMEM(pair_slots.shape[::-1], jnp.int32),
        pltpu.SMEM(pno_class.shape, jnp.int32),
        pltpu.VMEM(pno_energy.shape, jnp.float32),
        pltpu.SMEM(occ_energy.shape, jnp.float32),
        pltpu.VMEM((n_pair - 1, CHUNKS, 2, rows, half_mu), jnp.bfloat16),
        pltpu.VMEM((n_mine, mu, 2 * width), jnp.bfloat16),
        pltpu.VMEM((n_mine, 2 * width, width), jnp.bfloat16),
        pltpu.VMEM((n_mine, 2 * width, width), jnp.float32),
        pltpu.VMEM((n_mine, 2, width, width), jnp.bfloat16),
        pltpu.SMEM((need_lists.shape[1],), jnp.int32),
        dma((CHUNKS, n_pair - 1)),
        dma((CHUNKS, n_pair)),
    ]
    scratch += [dma((CHUNKS, n_pair)) for _ in range(6)]
    scratch += [dma((2, 2)), dma((8,)), dma((3, n_mine))]
    flops = 2 * n_occ * (2 * 2 * q_dev * mu * width + 2 * q_dev * width * width)
    return pl.pallas_call(
        functools.partial(kernel, n_pair),
        out_shape=jax.ShapeDtypeStruct(amplitudes.shape, jnp.bfloat16),
        in_specs=[hbm] * 8,
        out_specs=hbm,
        scratch_shapes=scratch,
        compiler_params=pltpu.CompilerParams(
            collective_id=0, has_side_effects=True, vmem_limit_bytes=60 * 1024 * 1024
        ),
        cost_estimate=pl.CostEstimate(flops=flops, bytes_accessed=8 * 1024 * 1024, transcendentals=0),
    )(blocks, need_lists, jnp.transpose(pair_slots), pno_class, projection, amplitudes, pno_energy, occ_energy)


def fits(mesh, blocks, need_lists, projection, amplitudes):
    n_pair = mesh.shape["pair"]
    if mesh.shape["aux"] != 2 or mesh.shape["sub"] != 2 or n_pair < 2:
        return False
    per_home, q_dev, half_mu = blocks.shape
    width = projection.shape[2]
    if amplitudes.shape[1:] != (width, width) or width % 128 or half_mu % 128 or q_dev % (16 * CHUNKS) or amplitudes.shape[0] % 2:
        return False
    held = 4 * 2 * n_pair * q_dev * half_mu * 2
    held += 2 * n_pair * q_dev * half_mu * 2 + 2 * projection.size * 2 + amplitudes.size * 10
    return held < 24 * 1024 * 1024


def solution(mesh):
    def one_device(blocks, need_lists, pair_slots, pno_class, projection, amplitudes, pno_energy, occ_energy):
        args = (blocks, need_lists, pair_slots, pno_class, projection, amplitudes, pno_energy, occ_energy)
        if fits(mesh, blocks, need_lists, projection, amplitudes):
            return gathered(mesh.shape["pair"], *args)
        return body(*args)

    placed = (
        P(("grp", "pair"), "aux", "sub"),
        P("grp", None),
        P(("grp", "pair"), None),
        P(("grp", "pair")),
        P(("grp", "pair"), None, "sub"),
        P(("grp", "pair"), "sub", "aux"),
        P(("grp", "pair"), None),
        P("grp"),
    )
    return jax.shard_map(
        one_device,
        mesh=mesh,
        in_specs=placed,
        out_specs=P(("grp", "pair"), "sub", "aux"),
        check_vma=False,
    )
```

```python
import functools

import jax
import jax.numpy as jnp
from jax import lax
from jax.experimental import pallas as pl
from jax.experimental.pallas import tpu as pltpu
from jax.sharding import PartitionSpec as P


def body(blocks, need_lists, pair_slots, pno_class, projection, amplitudes, pno_energy, occ_energy):
    owner = lax.axis_index("pair")
    wanted = lax.dynamic_index_in_dim(need_lists, owner, 0, keepdims=False)
    everything = lax.all_gather(blocks, "pair", axis=0, tiled=True)
    packed_pairs = jnp.take(everything, wanted, axis=0)
    whole = lax.all_gather(packed_pairs, "sub", axis=2, tiled=True)
    slot_i = pair_slots[:, 0]
    slot_j = pair_slots[:, 1]
    left_rows = jnp.take(whole, slot_i, axis=0)
    right_rows = jnp.take(whole, slot_j, axis=0)
    first_side = jnp.einsum(
        "ltb,lba->lta", left_rows, projection, preferred_element_type=jnp.float32
    ).astype(jnp.bfloat16)
    second_half = jnp.einsum(
        "ltb,lba->lta", right_rows, projection, preferred_element_type=jnp.float32
    ).astype(jnp.bfloat16)
    second_side = lax.all_gather(second_half, "sub", axis=2, tiled=True)
    summed = lax.psum_scatter(
        jnp.einsum("pqa,pqb->bpa", first_side, second_side, preferred_element_type=jnp.float32),
        "aux",
        scatter_dimension=0,
        tiled=True,
    )
    exchange_term = jnp.transpose(summed, (1, 2, 0))
    half_width = projection.shape[2]
    col_width = summed.shape[0]
    row_start = lax.axis_index("sub") * half_width
    col_start = lax.axis_index("aux") * col_width
    energy_rows = lax.dynamic_slice_in_dim(pno_energy, row_start, half_width, 1)
    energy_cols = lax.dynamic_slice_in_dim(pno_energy, col_start, col_width, 1)
    shift = jnp.take(occ_energy, jnp.take(wanted, slot_i)) + jnp.take(
        occ_energy, jnp.take(wanted, slot_j)
    )
    denominator = energy_rows[:, :, None] + energy_cols[:, None, :] - shift[:, None, None]
    npno = pno_energy.shape[1]
    live = npno // 4 * jnp.where(pno_class == 0, 1, jnp.where(pno_class == 1, 2, 4))
    row_mask_table = ((row_start + jnp.arange(half_width))[None, :] < live[:, None]).astype(
        jnp.float32
    )
    mask_cols = ((col_start + jnp.arange(col_width))[None, :] < live[:, None]).astype(jnp.float32)
    value = (
        row_mask_table[:, :, None]
        * mask_cols[:, None, :]
        * (exchange_term + denominator * amplitudes.astype(jnp.float32))
    )
    return value.astype(jnp.bfloat16)


SPLIT = (8, 8)
MESH = pl.DeviceIdType.MESH


def kernel(
    n_pair,
    blocks_hbm,
    need_hbm,
    slots_hbm,
    class_hbm,
    proj_ref,
    amp_ref,
    energy_hbm,
    occ_hbm,
    out_ref,
    *scratch,
):
    n_chunk = len(SPLIT)
    whole = scratch[:n_chunk]
    (blocks_ref, need_ref, slots_ref, class_ref, energy_ref, occ_ref, packed, basis, amp, acc,
     result, table, z_send, z_recv, x_send, x_recv, c_send, c_recv, d_send, d_recv, s_sem,
     l_sem, o_sem) = scratch[n_chunk:]
    home = lax.axis_index("pair")
    x = lax.axis_index("aux")
    c = lax.axis_index("sub")
    per_home, q_dev, half_mu = blocks_ref.shape
    need = need_ref.shape[1]
    unit = q_dev // 16
    size = [part * unit for part in SPLIT]
    begin = [sum(size[:t]) for t in range(n_chunk)]
    n_mine = basis.shape[0]
    width = out_ref.shape[2]
    mine = c * n_mine
    theirs = (1 - c) * n_mine
    here_cols = pl.ds(pl.multiple_of(c * width, width), width)

    def partner(off):
        place, bit = 0, 1
        while bit < n_pair:
            place = place + lax.rem(lax.div(home, bit) + off // bit, 2) * bit
            bit *= 2
        return place

    barrier = pltpu.get_barrier_semaphore()
    for off in range(1, n_pair):
        pl.semaphore_signal(
            barrier, inc=1, device_id={"pair": partner(off)}, device_id_type=MESH
        )
    pl.semaphore_signal(barrier, inc=1, device_id={"aux": 1 - x}, device_id_type=MESH)
    pl.semaphore_signal(barrier, inc=1, device_id={"sub": 1 - c}, device_id_type=MESH)

    loads = [
        pltpu.make_async_copy(source, target, l_sem.at[n])
        for n, (source, target) in enumerate(
            [
                (need_hbm, need_ref),
                (blocks_hbm, blocks_ref),
                (slots_hbm, slots_ref),
                (class_hbm, class_ref),
                (occ_hbm, occ_ref),
                (energy_hbm, energy_ref),
                (amp_ref.at[pl.ds(mine, n_mine)], amp.at[:, here_cols]),
                (proj_ref.at[pl.ds(mine, n_mine)], basis.at[:, :, here_cols]),
            ]
        )
    ]
    for load in loads:
        load.start()
    loads[0].wait()
    loads[1].wait()

    def pack(owner, store):
        seen = jnp.int32(0)
        local = [jnp.int32(0), jnp.int32(0)]
        for s in range(need):
            orbital = need_ref[owner, s] - home * per_home
            here = jnp.logical_and(orbital >= 0, orbital < per_home)
            for k in range(2):
                local[k] = jnp.where(jnp.logical_and(here, seen == k), orbital, local[k])
            seen = seen + here.astype(jnp.int32)
        for k in range(2):
            store(k, local[k])

    for off in range(1, n_pair):
        def store(k, index, off=off):
            packed[off - 1, k] = blocks_ref[index]
        pack(partner(off), store)

    def store_own(k, index):
        for t in range(n_chunk):
            whole[t][c, home * 2 + k, x] = blocks_ref[index, begin[t] : begin[t] + size[t], :]

    pack(home, store_own)

    pl.semaphore_wait(barrier, n_pair + 1)

    def z_copy(t, off):
        return pltpu.make_async_remote_copy(
            src_ref=packed.at[off - 1, :, pl.ds(begin[t], size[t])],
            dst_ref=whole[t].at[c, pl.ds(home * 2, 2), x],
            send_sem=z_send.at[t, off - 1],
            recv_sem=z_recv.at[t, home],
            device_id={"pair": partner(off)},
            device_id_type=MESH,
        )

    def z_wait(t, off):
        source = partner(off)
        place = whole[t].at[c, pl.ds(source * 2, 2), x]
        pltpu.make_async_remote_copy(
            src_ref=place,
            dst_ref=place,
            send_sem=z_send.at[t, off - 1],
            recv_sem=z_recv.at[t, source],
            device_id={"pair": source},
            device_id_type=MESH,
        ).wait_recv()

    def hop(t, off, axis, to, half, send, recv, core):
        source = partner(off)
        place = whole[t].at[core, pl.ds(source * 2, 2), half]
        return pltpu.make_async_remote_copy(
            src_ref=place,
            dst_ref=place,
            send_sem=send.at[t, source],
            recv_sem=recv.at[t, source],
            device_id={axis: to},
            device_id_type=MESH,
        )

    def x_out(t, off):
        return hop(t, off, "aux", 1 - x, x, x_send, x_recv, c)

    def x_in(t, off):
        return hop(t, off, "aux", 1 - x, 1 - x, x_send, x_recv, c)

    def c_out(t, off):
        return hop(t, off, "sub", 1 - c, x, c_send, c_recv, c)

    def c_in(t, off):
        return hop(t, off, "sub", 1 - c, x, c_send, c_recv, 1 - c)

    def d_out(t, off):
        return hop(t, off, "sub", 1 - c, 1 - x, d_send, d_recv, c)

    def d_in(t, off):
        return hop(t, off, "sub", 1 - c, 1 - x, d_send, d_recv, 1 - c)

    def swap(n, source, target):
        return pltpu.make_async_remote_copy(
            src_ref=source,
            dst_ref=target,
            send_sem=s_sem.at[n, 0],
            recv_sem=s_sem.at[n, 1],
            device_id={"sub": 1 - c},
            device_id_type=MESH,
        )

    for t in range(n_chunk):
        z_copy(t, 1).start()
    for t in range(n_chunk):
        for off in range(2, n_pair):
            z_copy(t, off).start()
    for t in range(n_chunk):
        x_out(t, 0).start()
    swaps = [
        swap(0, amp_ref.at[pl.ds(theirs, n_mine)], amp.at[:, here_cols]),
        swap(1, proj_ref.at[pl.ds(theirs, n_mine)], basis.at[:, :, here_cols]),
    ]
    for copy in swaps:
        copy.start()
    for t in range(n_chunk):
        c_out(t, 0).start()

    for s in range(need):
        orbital = need_ref[home, s]
        origin = lax.div(orbital, jnp.int32(per_home))
        rank = jnp.int32(0)
        for before in range(s):
            rank = rank + (lax.div(need_ref[home, before], jnp.int32(per_home)) == origin).astype(jnp.int32)
        table[s] = origin * 2 + jnp.minimum(rank, 1)

    for load in loads[2:]:
        load.wait()
    for copy in swaps:
        copy.wait()

    for i in range(n_mine):
        p = mine + i
        energy = jnp.where(c == 0, energy_ref[i : i + 1, :], energy_ref[n_mine + i : n_mine + i + 1, :])
        cols = jnp.where(x == 0, energy[:, :width], energy[:, width:])
        shift = occ_ref[need_ref[home, slots_ref[0, p]]] + occ_ref[need_ref[home, slots_ref[1, p]]]
        for half in range(2):
            part = slice(half * width, (half + 1) * width)
            down = jnp.transpose(jnp.broadcast_to(energy[:, part], (width, width)))
            acc[i, part] = (down + cols - shift) * amp[i, part].astype(jnp.float32)

    group = 5 if n_mine % 5 == 0 else 1

    def compute(t, i):
        p = mine + i
        slot_i = table[slots_ref[0, p]]
        slot_j = table[slots_ref[1, p]]
        rows = size[t]
        left = jnp.concatenate(
            [
                jnp.concatenate(
                    [whole[t][core, slot].reshape(2 * rows, half_mu) for core in range(2)], axis=1
                )
                for slot in (slot_i, slot_j)
            ],
            axis=0,
        )
        total = jnp.dot(left, basis[i], preferred_element_type=jnp.float32)
        first = total[: 2 * rows].astype(jnp.bfloat16)
        second = total[2 * rows :]
        second = jnp.where(x == 0, second[:, :width], second[:, width:]).astype(jnp.bfloat16)
        value = acc[i] + lax.dot_general(
            first, second, (((0,), (0,)), ((), ())), preferred_element_type=jnp.float32
        )
        if t < n_chunk - 1:
            acc[i] = value
            return
        kind = class_ref[p]
        live = jnp.where(kind == 0, width // 2, jnp.where(kind == 1, width, 2 * width))
        a = lax.broadcasted_iota(jnp.int32, value.shape, 0)
        b = lax.broadcasted_iota(jnp.int32, value.shape, 1) + x * width
        keep = jnp.logical_and(a < live, b < live)
        value = jnp.where(keep, value, 0.0).astype(out_ref.dtype)
        result[i, 0] = value[:width]
        result[i, 1] = value[width:]

    def keep_rows(g):
        return pltpu.make_async_copy(
            result.at[pl.ds(g * group, group), c],
            out_ref.at[pl.ds(mine + g * group, group)],
            o_sem.at[0, g],
        )

    def give_rows(g):
        return pltpu.make_async_remote_copy(
            src_ref=result.at[pl.ds(g * group, group), 1 - c],
            dst_ref=out_ref.at[pl.ds(mine + g * group, group)],
            send_sem=o_sem.at[1, g],
            recv_sem=o_sem.at[2, g],
            device_id={"sub": 1 - c},
            device_id_type=MESH,
        )

    def take_rows(g):
        place = out_ref.at[pl.ds(theirs + g * group, group)]
        return pltpu.make_async_remote_copy(
            src_ref=place,
            dst_ref=place,
            send_sem=o_sem.at[1, g],
            recv_sem=o_sem.at[2, g],
            device_id={"sub": 1 - c},
            device_id_type=MESH,
        )

    def compute_all(t):
        def step(g, carry):
            for u in range(group):
                compute(t, g * group + u)
            if t == n_chunk - 1:
                keep_rows(g).start()
                give_rows(g).start()
            return carry

        lax.fori_loop(0, n_mine // group, step, 0)

    def arrived(t):
        for off in range(n_pair):
            c_in(t, off).wait_recv()
            d_in(t, off).wait_recv()

    for t in range(n_chunk):
        z_wait(t, 1)
        x_out(t, 1).start()
        c_out(t, 1).start()
    for t in range(n_chunk):
        for off in range(n_pair):
            if off > 1:
                z_wait(t, off)
                x_out(t, off).start()
                c_out(t, off).start()
            if t:
                x_in(t - 1, off).wait_recv()
                d_out(t - 1, off).start()
        if t:
            arrived(t - 1)
            compute_all(t - 1)
    for off in range(n_pair):
        x_in(n_chunk - 1, off).wait_recv()
        d_out(n_chunk - 1, off).start()
    arrived(n_chunk - 1)
    compute_all(n_chunk - 1)

    for t in range(n_chunk):
        for off in range(n_pair):
            if off:
                z_copy(t, off).wait_send()
            x_out(t, off).wait_send()
            c_out(t, off).wait_send()
            d_out(t, off).wait_send()
    for g in range(n_mine // group):
        keep_rows(g).wait()
        give_rows(g).wait_send()
        take_rows(g).wait_recv()


def gathered(n_pair, blocks, need_lists, pair_slots, pno_class, projection, amplitudes, pno_energy, occ_energy):
    per_home, q_dev, half_mu = blocks.shape
    n_occ, mu, width = projection.shape
    unit = q_dev // 16
    dma = pltpu.SemaphoreType.DMA
    hbm = pl.BlockSpec(memory_space=pltpu.HBM)
    scratch = [pltpu.VMEM((2, 2 * n_pair, 2, part * unit, half_mu), jnp.bfloat16) for part in SPLIT]
    n_mine = n_occ // 2
    scratch += [
        pltpu.VMEM(blocks.shape, blocks.dtype),
        pltpu.SMEM(need_lists.shape, jnp.int32),
        pltpu.SMEM(pair_slots.shape[::-1], jnp.int32),
        pltpu.SMEM(pno_class.shape, jnp.int32),
        pltpu.VMEM(pno_energy.shape, jnp.float32),
        pltpu.SMEM(occ_energy.shape, jnp.float32),
        pltpu.VMEM((n_pair - 1, 2, q_dev, half_mu), jnp.bfloat16),
        pltpu.VMEM((n_mine, mu, 2 * width), jnp.bfloat16),
        pltpu.VMEM((n_mine, 2 * width, width), jnp.bfloat16),
        pltpu.VMEM((n_mine, 2 * width, width), jnp.float32),
        pltpu.VMEM((n_mine, 2, width, width), jnp.bfloat16),
        pltpu.SMEM((need_lists.shape[1],), jnp.int32),
        dma((len(SPLIT), n_pair - 1)),
        dma((len(SPLIT), n_pair)),
    ]
    scratch += [dma((len(SPLIT), n_pair)) for _ in range(6)]
    scratch += [dma((2, 2)), dma((8,)), dma((3, n_mine))]
    flops = 2 * n_occ * (2 * 2 * q_dev * mu * width + 2 * q_dev * width * width)
    return pl.pallas_call(
        functools.partial(kernel, n_pair),
        out_shape=jax.ShapeDtypeStruct(amplitudes.shape, jnp.bfloat16),
        in_specs=[hbm] * 8,
        out_specs=hbm,
        scratch_shapes=scratch,
        compiler_params=pltpu.CompilerParams(
            collective_id=0, has_side_effects=True, vmem_limit_bytes=60 * 1024 * 1024
        ),
        cost_estimate=pl.CostEstimate(flops=flops, bytes_accessed=8 * 1024 * 1024, transcendentals=0),
    )(blocks, need_lists, jnp.transpose(pair_slots), pno_class, projection, amplitudes, pno_energy, occ_energy)


def fits(mesh, blocks, need_lists, projection, amplitudes):
    n_pair = mesh.shape["pair"]
    if mesh.shape["aux"] != 2 or mesh.shape["sub"] != 2 or n_pair < 2 or n_pair & (n_pair - 1):
        return False
    per_home, q_dev, half_mu = blocks.shape
    width = projection.shape[2]
    if amplitudes.shape[1:] != (width, width) or width % 128 or half_mu % 128 or q_dev % 256 or amplitudes.shape[0] % 2:
        return False
    held = 4 * 2 * n_pair * q_dev * half_mu * 2
    held += 2 * n_pair * q_dev * half_mu * 2 + 2 * projection.size * 2 + amplitudes.size * 10
    return held < 24 * 1024 * 1024


def solution(mesh):
    def one_device(blocks, need_lists, pair_slots, pno_class, projection, amplitudes, pno_energy, occ_energy):
        args = (blocks, need_lists, pair_slots, pno_class, projection, amplitudes, pno_energy, occ_energy)
        if fits(mesh, blocks, need_lists, projection, amplitudes):
            return gathered(mesh.shape["pair"], *args)
        return body(*args)

    placed = (
        P(("grp", "pair"), "aux", "sub"),
        P("grp", None),
        P(("grp", "pair"), None),
        P(("grp", "pair")),
        P(("grp", "pair"), None, "sub"),
        P(("grp", "pair"), "sub", "aux"),
        P(("grp", "pair"), None),
        P("grp"),
    )
    return jax.shard_map(
        one_device,
        mesh=mesh,
        in_specs=placed,
        out_specs=P(("grp", "pair"), "sub", "aux"),
        check_vma=False,
    )
```
